32 devices in a mesh: grp: 2 (over y), tile: 4 (over z), shot: 2 (over x), gz: 2 (over core).
Axes of the slice: x: 2, y: 2, z: 4, core: 2. Of those that a mesh axis runs over, the one named last changes fastest.
Arguments:
- courant: float32 [128, 32, 256], P('tile', None, 'gz'), may hold values from 0.2 to 0.44
- forward_old: float32 [4, 128, 32, 256], P(('grp', 'shot'), 'tile', None, 'gz'), parts along dimension 0, may hold values from -6 to 6
- forward_now: float32 [4, 128, 32, 256], P(('grp', 'shot'), 'tile', None, 'gz'), parts along dimension 0, may hold values from -6 to 6
- adjoint_far: float32 [4, 128, 32, 256], P(('grp', 'shot'), 'tile', None, 'gz'), parts along dimension 0, may hold values from -6 to 6
- adjoint_near: float32 [4, 128, 32, 256], P(('grp', 'shot'), 'tile', None, 'gz'), parts along dimension 0, may hold values from -6 to 6
- wavelet: float32 [256], replicated, may hold values from 200 to 800
- source_cell: int32 [4], P(('grp', 'shot')), parts along dimension 0, may hold values from 0 to 1048575
- checkpoint_step: int32 [4], P(('grp', 'shot')), parts along dimension 0, may hold values from 0 to 255
- receiver_cell: int32 [4, 512], P(('grp', 'shot')), parts along dimension 0, may hold values from 0 to 1048575
- residual: float32 [4, 2, 512], P(('grp', 'shot')), parts along dimension 0, may hold values from -80 to 80
- weight_table: float32 [16], replicated, may hold values from 0.25 to 4
- weight_index: int32 [4], P(('grp', 'shot')), parts along dimension 0, may hold values from 0 to 15
Outputs:
- gradient: float32 [256, 32, 256], P(('grp', 'tile'), 'shot', 'gz'), parts along dimension 0
- illumination: float32 [256, 32, 256], P(('grp', 'tile'), 'shot', 'gz'), parts along dimension 0
- adjoint_now: float32 [4, 128, 32, 256], P(('grp', 'shot'), 'tile', None, 'gz'), parts along dimension 0
- adjoint_back: float32 [4, 128, 32, 256], P(('grp', 'shot'), 'tile', None, 'gz'), parts along dimension 0
The draws below stay inside these ranges and needn't reach their ends.
There are 2 independent parts, one for each index of `grp`. The reference program is written for one: setup_inputs(seed, part) draws one part's arguments, and reference() takes and returns one part's arrays. A program takes and returns all parts, laid end to end along the dimension named above; an argument that names none is the same for every part. Nothing has to cross between parts.
All inputs are finite; a program needn't handle non-finite values.
Results may differ from the reference program's by a relative error of at most 0.00002.
Values sent between devices are 32-bit elements; how exact they have to be, the bound alone decides.
A program may use at most 64 MiB of HBM per device.

```python
import math
import jax
import jax.numpy as jnp
from jax import lax

NY = 32
NREC = 512
NT = 256
NW = 16
NX = 128
NZ = 256
SHOTS = 2


def touch_ends(drawn, key, low, top_value):
    longest = drawn.shape.index(max(drawn.shape))
    spots = []
    for shift in (0, 1):
        where = [jax.random.randint(jax.random.fold_in(key, axis), (), 0, length) for axis, length in enumerate(drawn.shape)]
        where[longest] = (where[longest] + shift) % drawn.shape[longest]
        spots.append(tuple(where))
    return drawn.at[spots[0]].set(low).at[spots[1]].set(top_value)


def levels(stream_key, dims, shards, least, top_value):
    level, own = 1.0, jax.random.fold_in(stream_key, 6)
    for axis_at, parts in shards:
        steps = jnp.exp(jax.random.uniform(jax.random.fold_in(own, axis_at), (parts,), jnp.float32, least / len(shards), top_value / len(shards)))
        level = level * jnp.repeat(steps, dims[axis_at] // parts).reshape([-1 if axis == axis_at else 1 for axis in range(len(dims))])
    return level


def noise(stream_key, dims, scale, reach, shards=(), dtype=jnp.bfloat16):
    entries = jax.random.normal(stream_key, dims, jnp.float32) * scale
    if len(shards) > 0:
        entries = levels(stream_key, dims, shards, -0.22, 0.18) * entries
    return jnp.clip(entries, min=-reach, max=reach).astype(dtype)


def setup_inputs(seed: int = 0, part: int = 0) -> dict:
    splits = jax.random.split(jax.random.key(seed), 13)
    own_keys = jax.random.split(jax.random.fold_in(splits[12], part), 13)
    courant = jnp.clip(0.2 + 0.24 * jax.random.uniform(splits[0], (NX, NY, NZ), jnp.float32) ** levels(splits[0], (NX, NY, NZ), ((0, 4), (2, 2)), -0.2, 0.2), 0.2, 0.44)
    forward_old = noise(own_keys[1], (SHOTS, NX, NY, NZ), 1.0, 6.0, ((0, 2), (1, 4), (3, 2)), jnp.float32)
    forward_now = noise(own_keys[2], (SHOTS, NX, NY, NZ), 1.0, 6.0, ((0, 2), (1, 4), (3, 2)), jnp.float32)
    adjoint_far = noise(own_keys[3], (SHOTS, NX, NY, NZ), 1.0, 6.0, ((0, 2), (1, 4), (3, 2)), jnp.float32)
    adjoint_near = noise(own_keys[4], (SHOTS, NX, NY, NZ), 1.0, 6.0, ((0, 2), (1, 4), (3, 2)), jnp.float32)
    wavelet = jnp.clip(jax.random.uniform(splits[5], (NT,), jnp.float32, 200.0, 800.0), 200.0, 800.0)
    source_cell = jax.random.randint(own_keys[6], (SHOTS,), 0, NX * NY * NZ).astype(jnp.int32)
    checkpoint_step = jax.random.randint(own_keys[7], (SHOTS,), 0, NT).astype(jnp.int32)
    receiver_cell = touch_ends(jax.random.randint(own_keys[8], (SHOTS, NREC), 0, NX * NY * NZ), jax.random.fold_in(own_keys[8], 1), 0, (NX * NY * NZ) - 1).astype(jnp.int32)
    residual = jnp.clip(jax.random.uniform(own_keys[9], (SHOTS, 2, NREC), jnp.float32, -80.0, 80.0) * levels(own_keys[9], (SHOTS, 2, NREC), ((0, 2),), -0.4, 0.0), -80.0, 80.0)
    weight_table = jnp.clip(jnp.exp(jax.random.uniform(splits[10], (NW,), jnp.float32, math.log(0.25), math.log(4.0))), 0.25, 4.0)
    weight_index = jax.random.randint(own_keys[11], (SHOTS,), 0, NW).astype(jnp.int32)
    return {"courant": courant, "forward_old": forward_old, "forward_now": forward_now, "adjoint_far": adjoint_far, "adjoint_near": adjoint_near, "wavelet": wavelet, "source_cell": source_cell, "checkpoint_step": checkpoint_step, "receiver_cell": receiver_cell, "residual": residual, "weight_table": weight_table, "weight_index": weight_index}


STENCIL = (-205.0 / 72.0, 8.0 / 5.0, -1.0 / 5.0, 8.0 / 315.0, -1.0 / 560.0)


def laplace(field):
    padded = jnp.pad(field, 4)
    extent_x, extent_y, extent_z = field.shape
    center = padded[4:4 + extent_x, 4:4 + extent_y, 4:4 + extent_z]
    summed = 3.0 * STENCIL[0] * center
    for offset in range(1, 5):
        near_x = padded[4 + offset:4 + offset + extent_x, 4:4 + extent_y, 4:4 + extent_z] + padded[4 - offset:4 - offset + extent_x, 4:4 + extent_y, 4:4 + extent_z]
        near_y = padded[4:4 + extent_x, 4 + offset:4 + offset + extent_y, 4:4 + extent_z] + padded[4:4 + extent_x, 4 - offset:4 - offset + extent_y, 4:4 + extent_z]
        near_z = padded[4:4 + extent_x, 4:4 + extent_y, 4 + offset:4 + offset + extent_z] + padded[4:4 + extent_x, 4:4 + extent_y, 4 - offset:4 - offset + extent_z]
        summed = summed + STENCIL[offset] * (near_x + near_y + near_z)
    return summed


def spread(flat_cells, values):
    grid = jnp.zeros((NX * NY * NZ,), jnp.float32).at[flat_cells].add(values)
    return grid.reshape(NX, NY, NZ)


def reference(courant, forward_old, forward_now, adjoint_far, adjoint_near, wavelet, source_cell, checkpoint_step, receiver_cell, residual, weight_table, weight_index):
    speed_sq = courant * courant
    weights = weight_table[weight_index]

    def one_shot(shot_items):
        old_field, now_field, far_field, near_field, source, step, receivers, traces, weight = shot_items
        source_grid = spread(source[None], wavelet[step][None])
        lap_now = laplace(now_field)
        forward_next = 2.0 * now_field - old_field + speed_sq * (lap_now + source_grid)
        lap_next = laplace(forward_next)
        lap_near = laplace(near_field)
        adjoint_now = 2.0 * near_field - far_field + speed_sq * (lap_near + spread(receivers, traces[0]))
        lap_adjoint = laplace(adjoint_now)
        adjoint_back = 2.0 * adjoint_now - near_field + speed_sq * (lap_adjoint + spread(receivers, traces[1]))
        grad_term = weight * 2.0 * courant * (near_field * lap_next + adjoint_now * lap_now)
        energy_term = weight * (forward_next * forward_next + now_field * now_field)
        return adjoint_now, adjoint_back, grad_term, energy_term

    adjoint_now, adjoint_back, grad_terms, energy_terms = lax.map(one_shot, (forward_old, forward_now, adjoint_far, adjoint_near, source_cell, checkpoint_step, receiver_cell, residual, weights))
    gradient = jnp.sum(grad_terms, axis=0) / SHOTS
    illumination = jnp.sum(energy_terms, axis=0) / SHOTS
    return gradient, illumination, adjoint_now, adjoint_back
```

```python
import functools

import jax
import jax.numpy as jnp
import ml_dtypes
import numpy as np
from jax import lax
from jax.experimental import pallas as pl
from jax.experimental.pallas import tpu as pltpu
from jax.sharding import PartitionSpec as P

STENCIL = (-205.0 / 72.0, 8.0 / 5.0, -1.0 / 5.0, 8.0 / 315.0, -1.0 / 560.0)
HIGH = tuple(float(np.float32(c).astype(ml_dtypes.bfloat16)) for c in STENCIL)
LOW = tuple(float(np.float32(c - h).astype(ml_dtypes.bfloat16)) for c, h in zip(STENCIL, HIGH))
MESH = pl.DeviceIdType.MESH
PAD = 8
HALO = 4
ENERGY_CHUNKS = ((4, 16), (16, 28), (0, 4), (28, 32))
GRAD_CHUNKS = ((8, 16), (16, 24), (0, 8), (24, 32))


def kernel(
    sizes,
    courant_hbm, old_hbm, now_hbm, far_hbm, near_hbm,
    wavelet, source_cell, step, cells, residual, table, index,
    grad_hbm, energy_hbm, anow_hbm, aback_hbm,
    fpad, apad, fpad2, apad2, courant, old, far, zf, za, lapf, rec0, rec1, back,
    ebuf, gbuf, erecv, grecv, band, qsend, qrecv, hot,
    in_sem, out_sem, face_send, face_recv, zsend, zrecv, esend_sem, erecv_sem, gsend_sem, grecv_sem,
):
    tiles, shots, nx, ny, nz = sizes
    rows_y = ny // shots
    total_z = 2 * nz
    tile, shot, gz = (lax.axis_index(a) for a in ("tile", "shot", "gz"))
    y0, y1 = PAD, PAD + ny

    def inner(ref):
        return ref.at[HALO:HALO + nx, y0:y1, :]

    loads = [
        pltpu.make_async_copy(now_hbm.at[0], inner(fpad), in_sem.at[0]),
        pltpu.make_async_copy(near_hbm.at[0], inner(apad), in_sem.at[1]),
        pltpu.make_async_copy(old_hbm.at[0], old, in_sem.at[2]),
        pltpu.make_async_copy(courant_hbm, courant, in_sem.at[3]),
        pltpu.make_async_copy(far_hbm.at[0], far, in_sem.at[4]),
    ]
    for load in loads:
        load.start()

    barrier = pltpu.get_barrier_semaphore()
    pl.semaphore_signal(barrier, 1, device_id={"gz": 1 - gz}, device_id_type=MESH)
    for d in range(1, shots):
        pl.semaphore_signal(barrier, 1, device_id={"shot": lax.rem(shot + d, shots)}, device_id_type=MESH)

    @pl.when(tile > 0)
    def _():
        pl.semaphore_signal(barrier, 1, device_id={"tile": tile - 1}, device_id_type=MESH)

    @pl.when(tile < tiles - 1)
    def _():
        pl.semaphore_signal(barrier, 1, device_id={"tile": tile + 1}, device_id_type=MESH)

    for ref in (fpad, apad, fpad2, apad2):
        def clear(x, _, ref=ref):
            ref[x + HALO, 0:PAD, :] = jnp.zeros((PAD, nz), jnp.float32)
            ref[x + HALO, y1:y1 + PAD, :] = jnp.zeros((PAD, nz), jnp.float32)
            return 0
        lax.fori_loop(0, nx, clear, 0)

        @pl.when(tile == 0)
        def _():
            ref[0:HALO, y0:y1, :] = jnp.zeros((HALO, ny, nz), jnp.float32)

        @pl.when(tile == tiles - 1)
        def _():
            ref[HALO + nx:, y0:y1, :] = jnp.zeros((HALO, ny, nz), jnp.float32)

    ki = lax.broadcasted_iota(jnp.int32, (nz, nz), 0)
    kj = lax.broadcasted_iota(jnp.int32, (nz, nz), 1)
    dist = jnp.abs(ki - kj)
    upper = jnp.zeros((nz, nz), jnp.float32)
    lower = jnp.zeros((nz, nz), jnp.float32)
    for k in range(1, 5):
        upper = jnp.where(dist == k, HIGH[k], upper)
        lower = jnp.where(dist == k, LOW[k], lower)
    band[0:nz, 0:nz] = upper.astype(jnp.bfloat16)
    band[nz:2 * nz, 0:nz] = upper.astype(jnp.bfloat16)
    band[0:nz, nz:2 * nz] = lower.astype(jnp.bfloat16)
    band[nz:2 * nz, nz:2 * nz] = jnp.zeros((nz, nz), jnp.bfloat16)

    weight = table[index[0]] / shots
    amplitude = wavelet[step[0]]
    cell = source_cell[0]
    z_bits = total_z.bit_length() - 1
    y_bits = ny.bit_length() - 1
    src_row = lax.shift_right_logical(cell, z_bits)
    src_z = (cell & (total_z - 1)) - gz * nz
    src_y = src_row & (ny - 1)
    src_x = lax.shift_right_logical(src_row, y_bits) - tile * nx
    lane = lax.broadcasted_iota(jnp.int32, (ny, nz), 1)
    sub = lax.broadcasted_iota(jnp.int32, (ny, nz), 0)
    src_plane = jnp.where((sub == src_y) & (lane == src_z), amplitude, 0.0)
    first_edge = jnp.where(gz == 0, nz - HALO, 0)
    edge = (lane >= first_edge) & (lane < first_edge + HALO)
    quad = lax.shift_right_logical(lane, 2)
    place = lane & 3

    rc = cells[...]
    rec_row = lax.shift_right_logical(rc, z_bits) - tile * (nx * ny)
    rec_z = (rc & (total_z - 1)) - gz * nz
    nrec = rc.shape[1]
    z_hot = lax.broadcasted_iota(jnp.int32, (nz, nrec), 0) == rec_z
    for j in range(2):
        res = residual[0, j:j + 1, :]
        res_hi = res.astype(jnp.bfloat16).astype(jnp.float32)
        res_lo = res - res_hi
        hot[(2 * j) * nz:(2 * j + 1) * nz, :] = jnp.where(z_hot, res_hi, 0.0).astype(jnp.bfloat16)
        hot[(2 * j + 1) * nz:(2 * j + 2) * nz, :] = jnp.where(z_hot, res_lo, 0.0).astype(jnp.bfloat16)

    def face(n, ref, up):
        if up:
            src, dst, peer = ref.at[nx:nx + HALO, y0:y1, :], ref.at[0:HALO, y0:y1, :], tile + 1
        else:
            src, dst, peer = ref.at[HALO:2 * HALO, y0:y1, :], ref.at[HALO + nx:, y0:y1, :], tile - 1
        i = 2 * n + int(up)
        return pltpu.make_async_remote_copy(
            src_ref=src, dst_ref=dst, send_sem=face_send.at[i], recv_sem=face_recv.at[i],
            device_id={"tile": peer}, device_id_type=MESH)

    def send_faces(n, ref):
        @pl.when(tile < tiles - 1)
        def _():
            face(n, ref, True).start()

        @pl.when(tile > 0)
        def _():
            face(n, ref, False).start()

    def recv_faces(n, ref):
        @pl.when(tile > 0)
        def _():
            face(n, ref, True).wait_recv()

        @pl.when(tile < tiles - 1)
        def _():
            face(n, ref, False).wait_recv()

    def sent_faces(n, ref):
        @pl.when(tile < tiles - 1)
        def _():
            face(n, ref, True).wait_send()

        @pl.when(tile > 0)
        def _():
            face(n, ref, False).wait_send()

    def sides(n):
        return pltpu.make_async_remote_copy(
            src_ref=qsend.at[n], dst_ref=qrecv.at[n], send_sem=zsend.at[n], recv_sem=zrecv.at[n],
            device_id={"gz": 1 - gz}, device_id_type=MESH)

    def sums(buf, landing, send, recv, chunks, i, d):
        a, b = chunks[i]
        peer = lax.rem(shot + d, shots)
        return pltpu.make_async_remote_copy(
            src_ref=buf.at[peer, a:b], dst_ref=landing.at[d - 1, a:b],
            send_sem=send.at[i, d - 1], recv_sem=recv.at[i, d - 1],
            device_id={"shot": peer}, device_id_type=MESH)

    energy = functools.partial(sums, ebuf, erecv, esend_sem, erecv_sem, ENERGY_CHUNKS)
    grads = functools.partial(sums, gbuf, grecv, gsend_sem, grecv_sem, GRAD_CHUNKS)

    def pack(n, ref):
        def body(x, acc):
            plane = ref[x + HALO, y0:y1, :]
            turned = pltpu.roll(plane, (4 * x + jnp.where(gz == 0, 4, 0)) & (nz - 1), 1)
            return jnp.where(quad == x, turned, acc)
        packed = lax.fori_loop(0, nx, body, jnp.zeros((ny, nz), jnp.float32), unroll=4)
        total = STENCIL[4] * packed
        for d in range(1, 4):
            shift = jnp.where(gz == 1, d, nz - d)
            valid = jnp.where(gz == 1, place, 3 - place) >= d
            total = total + jnp.where(valid, STENCIL[4 - d] * pltpu.roll(packed, shift, 1), 0.0)
        qsend[n] = total
        sides(n).start()

    def along_z(ref, out, chunk=8):
        def body(i, _):
            x = i * chunk
            v = ref[pl.ds(HALO + x, chunk), y0:y1, :].reshape(chunk * ny, nz)
            hi = v.astype(jnp.bfloat16)
            lo = (v - hi.astype(jnp.float32)).astype(jnp.bfloat16)
            both = jnp.concatenate([hi, lo], axis=1)
            res = jnp.dot(both, band[...], preferred_element_type=jnp.float32)
            out[pl.ds(x, chunk)] = (res[:, :nz] + res[:, nz:]).reshape(chunk, ny, nz)
            return 0
        lax.fori_loop(0, nx // chunk, body, 0, unroll=2)

    def laplace(ref, zpart, q, x):
        centre = ref[x + HALO, y0:y1, :]
        turned = pltpu.roll(q, (first_edge - 4 * x + nz) & (nz - 1), 1)
        acc = zpart[x] + jnp.where(edge, turned, 0.0) + (3.0 * STENCIL[0]) * centre
        for k in range(1, 5):
            near = (ref[x + HALO - k, y0:y1, :] + ref[x + HALO + k, y0:y1, :]) + (
                ref[x + HALO, y0 - k:y1 - k, :] + ref[x + HALO, y0 + k:y1 + k, :])
            acc = acc + STENCIL[k] * near
        return acc, centre

    def planes(body, a, b):
        def step_fn(x, _):
            body(x)
            return 0
        lax.fori_loop(a, b, step_fn, 0, unroll=2)

    loads[0].wait()
    pl.semaphore_wait(
        barrier, shots + jnp.where(tile > 0, 1, 0) + jnp.where(tile < tiles - 1, 1, 0))

    send_faces(0, fpad)
    pack(0, fpad)
    loads[1].wait()
    send_faces(1, apad)
    pack(1, apad)
    along_z(fpad, zf)
    loads[2].wait()
    loads[3].wait()
    sides(0).wait_recv()
    q0 = qrecv[0]

    def forward(x):
        lap, now = laplace(fpad, zf, q0, x)
        lapf[x] = lap
        c = courant[x]
        src = src_plane * jnp.where(x == src_x, 1.0, 0.0)
        nxt = 2.0 * now - old[x] + (c * c) * (lap + src)
        fpad2[x + HALO, y0:y1, :] = nxt
        e = weight * (nxt * nxt + now * now)
        for s in range(shots):
            ebuf[s, x] = e[s * rows_y:(s + 1) * rows_y, :]

    for i in range(2):
        planes(forward, *ENERGY_CHUNKS[i])
        for d in range(1, shots):
            energy(i, d).start()
    recv_faces(0, fpad)
    for i in range(2, 4):
        planes(forward, *ENERGY_CHUNKS[i])
        for d in range(1, shots):
            energy(i, d).start()
    send_faces(2, fpad2)
    pack(2, fpad2)

    along_z(apad, za)
    chunk_rows = 256

    def receivers(i, _):
        base = i * chunk_rows
        row = lax.broadcasted_iota(jnp.int32, (chunk_rows, nrec), 0) + base
        row_hot = jnp.where(row == rec_row, 1.0, 0.0).astype(jnp.bfloat16)
        res = lax.dot_general(row_hot, hot[...], (((1,), (1,)), ((), ())), preferred_element_type=jnp.float32)
        px = chunk_rows // ny
        rec0[pl.ds(i * px, px)] = (res[:, :nz] + res[:, nz:2 * nz]).reshape(px, ny, nz)
        rec1[pl.ds(i * px, px)] = (res[:, 2 * nz:3 * nz] + res[:, 3 * nz:]).reshape(px, ny, nz)
        return 0

    lax.fori_loop(0, nx * ny // chunk_rows, receivers, 0)
    loads[4].wait()
    sides(1).wait_recv()
    recv_faces(1, apad)
    q1 = qrecv[1]

    def adjoint(x):
        lap, near = laplace(apad, za, q1, x)
        c = courant[x]
        apad2[x + HALO, y0:y1, :] = 2.0 * near - far[x] + (c * c) * (lap + rec0[x])

    planes(adjoint, 0, 4)
    planes(adjoint, nx - 4, nx)
    send_faces(3, apad2)
    planes(adjoint, 4, nx - 4)
    pack(3, apad2)
    store_now = pltpu.make_async_copy(inner(apad2), anow_hbm.at[0], out_sem.at[0])
    store_now.start()

    along_z(fpad2, zf)
    sides(2).wait_recv()
    q2 = qrecv[2]

    def gradient(x):
        lap, _ = laplace(fpad2, zf, q2, x)
        g = (2.0 * weight) * courant[x] * (
            apad[x + HALO, y0:y1, :] * lap + apad2[x + HALO, y0:y1, :] * lapf[x])
        for s in range(shots):
            gbuf[s, x] = g[s * rows_y:(s + 1) * rows_y, :]

    for i in range(2):
        planes(gradient, *GRAD_CHUNKS[i])
        for d in range(1, shots):
            grads(i, d).start()
    recv_faces(2, fpad2)
    for i in range(2, 4):
        planes(gradient, *GRAD_CHUNKS[i])
        for d in range(1, shots):
            grads(i, d).start()

    along_z(apad2, za)
    sides(3).wait_recv()
    recv_faces(3, apad2)
    q3 = qrecv[3]

    def adjoint_back(x):
        lap, now = laplace(apad2, za, q3, x)
        c = courant[x]
        back[x] = 2.0 * now - apad[x + HALO, y0:y1, :] + (c * c) * (lap + rec1[x])

    planes(adjoint_back, 0, nx)
    store_back = pltpu.make_async_copy(back, aback_hbm.at[0], out_sem.at[1])
    store_back.start()

    stores = []
    for n, (buf, landing, copies, chunks, out) in enumerate((
            (ebuf, erecv, energy, ENERGY_CHUNKS, energy_hbm),
            (gbuf, grecv, grads, GRAD_CHUNKS, grad_hbm))):
        for i, (a, b) in enumerate(chunks):
            for d in range(1, shots):
                copies(i, d).wait_recv()

            def total(x, buf=buf, landing=landing):
                acc = buf[shot, x]
                for d in range(1, shots):
                    acc = acc + landing[d - 1, x]
                landing[0, x] = acc

            planes(total, a, b)
            store = pltpu.make_async_copy(landing.at[0, a:b], out.at[a:b], out_sem.at[2 + 4 * n + i])
            store.start()
            stores.append(store)

    for n, ref in enumerate((fpad, apad, fpad2, apad2)):
        sent_faces(n, ref)
        sides(n).wait_send()
    for i in range(4):
        for d in range(1, shots):
            energy(i, d).wait_send()
            grads(i, d).wait_send()
    store_now.wait()
    store_back.wait()
    for store in stores:
        store.wait()


def shards(tiles, shots, *args):
    _, nx, ny, nz = args[2].shape
    nrec = args[8].shape[1]
    rows_y = ny // shots
    landings = max(shots - 1, 1)
    block = (nx, ny, nz)
    padded = (nx + 2 * HALO, ny + 2 * PAD, nz)
    f32 = jnp.float32
    anywhere = pl.BlockSpec(memory_space=pl.ANY)
    vmem = pl.BlockSpec(memory_space=pltpu.VMEM)
    smem = pl.BlockSpec(memory_space=pltpu.SMEM)
    dma = pltpu.SemaphoreType.DMA
    return pl.pallas_call(
        functools.partial(kernel, (tiles, shots, nx, ny, nz)),
        out_shape=(
            jax.ShapeDtypeStruct((nx, rows_y, nz), f32),
            jax.ShapeDtypeStruct((nx, rows_y, nz), f32),
            jax.ShapeDtypeStruct((1,) + block, f32),
            jax.ShapeDtypeStruct((1,) + block, f32),
        ),
        in_specs=[anywhere] * 5 + [smem] * 3 + [vmem] * 2 + [smem] * 2,
        out_specs=(anywhere,) * 4,
        scratch_shapes=(
            [pltpu.VMEM(padded, f32)] * 4
            + [pltpu.VMEM(block, f32)] * 9
            + [pltpu.VMEM((shots, nx, rows_y, nz), f32)] * 2
            + [pltpu.VMEM((landings, nx, rows_y, nz), f32)] * 2
            + [
                pltpu.VMEM((2 * nz, 2 * nz), jnp.bfloat16),
                pltpu.VMEM((4, ny, nz), f32),
                pltpu.VMEM((4, ny, nz), f32),
                pltpu.VMEM((4 * nz, nrec), jnp.bfloat16),
                dma((5,)), dma((10,)), dma((8,)), dma((8,)), dma((4,)), dma((4,)),
                dma((4, landings)), dma((4, landings)), dma((4, landings)), dma((4, landings)),
            ]
        ),
        compiler_params=pltpu.CompilerParams(
            collective_id=0, has_side_effects=True, vmem_limit_bytes=48 * 1024 * 1024),
        cost_estimate=pl.CostEstimate(
            flops=130 * nx * ny * nz, bytes_accessed=32 * nx * ny * nz, transcendentals=0),
        name="adjoint_window",
    )(*args)


def solution(mesh):
    wave = P(("grp", "shot"), "tile", None, "gz")
    one = P(("grp", "shot"))
    in_specs = (P("tile", None, "gz"), wave, wave, wave, wave, P(), one, one,
                P(("grp", "shot"), None), P(("grp", "shot"), None, None), P(), one)
    out_specs = (P(("grp", "tile"), "shot", "gz"), P(("grp", "tile"), "shot", "gz"), wave, wave)
    body = functools.partial(shards, mesh.shape["tile"], mesh.shape["shot"])
    return jax.shard_map(body, mesh=mesh, in_specs=in_specs, out_specs=out_specs, check_vma=False)
```

```python
import functools

import jax
import jax.numpy as jnp
import ml_dtypes
import numpy as np
from jax import lax
from jax.experimental import pallas as pl
from jax.experimental.pallas import tpu as pltpu
from jax.sharding import PartitionSpec as P

STENCIL = (-205.0 / 72.0, 8.0 / 5.0, -1.0 / 5.0, 8.0 / 315.0, -1.0 / 560.0)
HIGH = tuple(float(np.float32(c).astype(ml_dtypes.bfloat16)) for c in STENCIL)
LOW = tuple(float(np.float32(c - h).astype(ml_dtypes.bfloat16)) for c, h in zip(STENCIL, HIGH))
MESH = pl.DeviceIdType.MESH
PAD = 8
HALO = 4
ENERGY_CHUNKS = ((4, 16), (16, 28), (0, 4), (28, 32))
GRAD_CHUNKS = ((8, 16), (16, 24), (0, 8), (24, 32))


def kernel(
    sizes,
    courant_hbm, old_hbm, now_hbm, far_hbm, near_hbm,
    wavelet_hbm, scalars_hbm, cells_hbm, residual_hbm, table_hbm,
    grad_hbm, energy_hbm, anow_hbm, aback_hbm,
    fpad, apad, fpad2, apad2, courant, old, far, zf, za, lapf, rec0, rec1, back,
    ebuf, gbuf, erecv, grecv, band, qsend, qrecv, hot,
    wavelet, scalars, cells, residual, table,
    in_sem, out_sem, face_send, face_recv, zsend, zrecv, esend_sem, erecv_sem, gsend_sem, grecv_sem,
):
    tiles, shots, nx, ny, nz = sizes
    rows_y = ny // shots
    total_z = 2 * nz
    tile, shot, gz = (lax.axis_index(a) for a in ("tile", "shot", "gz"))
    y0, y1 = PAD, PAD + ny

    def inner(ref):
        return ref.at[HALO:HALO + nx, y0:y1, :]

    loads = [
        pltpu.make_async_copy(now_hbm.at[0], inner(fpad), in_sem.at[0]),
        pltpu.make_async_copy(near_hbm.at[0], inner(apad), in_sem.at[1]),
        pltpu.make_async_copy(old_hbm.at[0], old, in_sem.at[2]),
        pltpu.make_async_copy(courant_hbm, courant, in_sem.at[3]),
        pltpu.make_async_copy(far_hbm.at[0], far, in_sem.at[4]),
    ]
    small = [
        pltpu.make_async_copy(src, dst, in_sem.at[5 + i])
        for i, (src, dst) in enumerate((
            (wavelet_hbm, wavelet), (scalars_hbm, scalars), (cells_hbm, cells),
            (residual_hbm, residual), (table_hbm, table)))
    ]
    for load in loads[:2] + small + loads[2:]:
        load.start()

    barrier = pltpu.get_barrier_semaphore()
    pl.semaphore_signal(barrier, 1, device_id={"gz": 1 - gz}, device_id_type=MESH)
    for d in range(1, shots):
        pl.semaphore_signal(barrier, 1, device_id={"shot": lax.rem(shot + d, shots)}, device_id_type=MESH)

    @pl.when(tile > 0)
    def _():
        pl.semaphore_signal(barrier, 1, device_id={"tile": tile - 1}, device_id_type=MESH)

    @pl.when(tile < tiles - 1)
    def _():
        pl.semaphore_signal(barrier, 1, device_id={"tile": tile + 1}, device_id_type=MESH)

    for ref in (fpad, apad, fpad2, apad2):
        def clear(x, _, ref=ref):
            ref[x + HALO, 0:PAD, :] = jnp.zeros((PAD, nz), jnp.float32)
            ref[x + HALO, y1:y1 + PAD, :] = jnp.zeros((PAD, nz), jnp.float32)
            return 0
        lax.fori_loop(0, nx, clear, 0, unroll=8)

        @pl.when(tile == 0)
        def _():
            ref[0:HALO, y0:y1, :] = jnp.zeros((HALO, ny, nz), jnp.float32)

        @pl.when(tile == tiles - 1)
        def _():
            ref[HALO + nx:, y0:y1, :] = jnp.zeros((HALO, ny, nz), jnp.float32)

    ki = lax.broadcasted_iota(jnp.int32, (nz, nz), 0)
    kj = lax.broadcasted_iota(jnp.int32, (nz, nz), 1)
    dist = jnp.abs(ki - kj)
    upper = jnp.zeros((nz, nz), jnp.float32)
    lower = jnp.zeros((nz, nz), jnp.float32)
    for k in range(1, 5):
        upper = jnp.where(dist == k, HIGH[k], upper)
        lower = jnp.where(dist == k, LOW[k], lower)
    band[0:nz, 0:nz] = upper.astype(jnp.bfloat16)
    band[nz:2 * nz, 0:nz] = upper.astype(jnp.bfloat16)
    band[0:nz, nz:2 * nz] = lower.astype(jnp.bfloat16)
    band[nz:2 * nz, nz:2 * nz] = jnp.zeros((nz, nz), jnp.bfloat16)

    for load in small:
        load.wait()
    weight = table[scalars[2]] / shots
    amplitude = wavelet[scalars[1]]
    cell = scalars[0]
    z_bits = total_z.bit_length() - 1
    y_bits = ny.bit_length() - 1
    src_row = lax.shift_right_logical(cell, z_bits)
    src_z = (cell & (total_z - 1)) - gz * nz
    src_y = src_row & (ny - 1)
    src_x = lax.shift_right_logical(src_row, y_bits) - tile * nx
    lane = lax.broadcasted_iota(jnp.int32, (ny, nz), 1)
    sub = lax.broadcasted_iota(jnp.int32, (ny, nz), 0)
    src_plane = jnp.where((sub == src_y) & (lane == src_z), amplitude, 0.0)
    first_edge = jnp.where(gz == 0, nz - HALO, 0)
    edge = (lane >= first_edge) & (lane < first_edge + HALO)
    quad = lax.shift_right_logical(lane, 2)
    place = lane & 3

    rc = cells[...]
    rec_row = lax.shift_right_logical(rc, z_bits) - tile * (nx * ny)
    rec_z = (rc & (total_z - 1)) - gz * nz
    nrec = rc.shape[1]
    z_hot = lax.broadcasted_iota(jnp.int32, (nz, nrec), 0) == rec_z
    for j in range(2):
        res = residual[0, j:j + 1, :]
        res_hi = res.astype(jnp.bfloat16).astype(jnp.float32)
        res_lo = res - res_hi
        hot[(2 * j) * nz:(2 * j + 1) * nz, :] = jnp.where(z_hot, res_hi, 0.0).astype(jnp.bfloat16)
        hot[(2 * j + 1) * nz:(2 * j + 2) * nz, :] = jnp.where(z_hot, res_lo, 0.0).astype(jnp.bfloat16)

    def face(n, ref, up):
        if up:
            src, dst, peer = ref.at[nx:nx + HALO, y0:y1, :], ref.at[0:HALO, y0:y1, :], tile + 1
        else:
            src, dst, peer = ref.at[HALO:2 * HALO, y0:y1, :], ref.at[HALO + nx:, y0:y1, :], tile - 1
        i = 2 * n + int(up)
        return pltpu.make_async_remote_copy(
            src_ref=src, dst_ref=dst, send_sem=face_send.at[i], recv_sem=face_recv.at[i],
            device_id={"tile": peer}, device_id_type=MESH)

    def send_faces(n, ref):
        @pl.when(tile < tiles - 1)
        def _():
            face(n, ref, True).start()

        @pl.when(tile > 0)
        def _():
            face(n, ref, False).start()

    def recv_faces(n, ref):
        @pl.when(tile > 0)
        def _():
            face(n, ref, True).wait_recv()

        @pl.when(tile < tiles - 1)
        def _():
            face(n, ref, False).wait_recv()

    def sent_faces(n, ref):
        @pl.when(tile < tiles - 1)
        def _():
            face(n, ref, True).wait_send()

        @pl.when(tile > 0)
        def _():
            face(n, ref, False).wait_send()

    def sides(n):
        return pltpu.make_async_remote_copy(
            src_ref=qsend.at[n], dst_ref=qrecv.at[n], send_sem=zsend.at[n], recv_sem=zrecv.at[n],
            device_id={"gz": 1 - gz}, device_id_type=MESH)

    def sums(buf, landing, send, recv, chunks, i, d):
        a, b = chunks[i]
        peer = lax.rem(shot + d, shots)
        return pltpu.make_async_remote_copy(
            src_ref=buf.at[peer, a:b], dst_ref=landing.at[d - 1, a:b],
            send_sem=send.at[i, d - 1], recv_sem=recv.at[i, d - 1],
            device_id={"shot": peer}, device_id_type=MESH)

    energy = functools.partial(sums, ebuf, erecv, esend_sem, erecv_sem, ENERGY_CHUNKS)
    grads = functools.partial(sums, gbuf, grecv, gsend_sem, grecv_sem, GRAD_CHUNKS)

    def pack(n, ref):
        def body(x, acc):
            plane = ref[x + HALO, y0:y1, :]
            turned = pltpu.roll(plane, (4 * x + jnp.where(gz == 0, 4, 0)) & (nz - 1), 1)
            return jnp.where(quad == x, turned, acc)
        packed = lax.fori_loop(0, nx, body, jnp.zeros((ny, nz), jnp.float32), unroll=16)
        total = STENCIL[4] * packed
        for d in range(1, 4):
            shift = jnp.where(gz == 1, d, nz - d)
            valid = jnp.where(gz == 1, place, 3 - place) >= d
            total = total + jnp.where(valid, STENCIL[4 - d] * pltpu.roll(packed, shift, 1), 0.0)
        qsend[n] = total
        sides(n).start()

    def along_z(ref, out, chunk=8):
        def body(i, _):
            x = i * chunk
            v = ref[pl.ds(HALO + x, chunk), y0:y1, :].reshape(chunk * ny, nz)
            hi = v.astype(jnp.bfloat16)
            lo = (v - hi.astype(jnp.float32)).astype(jnp.bfloat16)
            both = jnp.concatenate([hi, lo], axis=1)
            res = jnp.dot(both, band[...], preferred_element_type=jnp.float32)
            out[pl.ds(x, chunk)] = (res[:, :nz] + res[:, nz:]).reshape(chunk, ny, nz)
            return 0
        lax.fori_loop(0, nx // chunk, body, 0, unroll=4)

    def laplace(ref, zpart, q, x):
        centre = ref[x + HALO, y0:y1, :]
        turned = pltpu.roll(q, (first_edge - 4 * x + nz) & (nz - 1), 1)
        acc = zpart[x] + jnp.where(edge, turned, 0.0) + (3.0 * STENCIL[0]) * centre
        for k in range(1, 5):
            near = (ref[x + HALO - k, y0:y1, :] + ref[x + HALO + k, y0:y1, :]) + (
                ref[x + HALO, y0 - k:y1 - k, :] + ref[x + HALO, y0 + k:y1 + k, :])
            acc = acc + STENCIL[k] * near
        return acc, centre

    def planes(body, a, b):
        def step_fn(x, _):
            body(x)
            return 0
        lax.fori_loop(a, b, step_fn, 0, unroll=4)

    loads[0].wait()
    pl.semaphore_wait(
        barrier, shots + jnp.where(tile > 0, 1, 0) + jnp.where(tile < tiles - 1, 1, 0))

    send_faces(0, fpad)
    pack(0, fpad)
    loads[1].wait()
    send_faces(1, apad)
    pack(1, apad)
    along_z(fpad, zf)
    loads[2].wait()
    loads[3].wait()
    sides(0).wait_recv()
    q0 = qrecv[0]

    def forward(x):
        lap, now = laplace(fpad, zf, q0, x)
        lapf[x] = lap
        c = courant[x]
        src = src_plane * jnp.where(x == src_x, 1.0, 0.0)
        nxt = 2.0 * now - old[x] + (c * c) * (lap + src)
        fpad2[x + HALO, y0:y1, :] = nxt
        e = weight * (nxt * nxt + now * now)
        for s in range(shots):
            ebuf[s, x] = e[s * rows_y:(s + 1) * rows_y, :]

    for i in range(2):
        planes(forward, *ENERGY_CHUNKS[i])
        for d in range(1, shots):
            energy(i, d).start()
    recv_faces(0, fpad)
    for i in range(2, 4):
        planes(forward, *ENERGY_CHUNKS[i])
        for d in range(1, shots):
            energy(i, d).start()
    send_faces(2, fpad2)
    pack(2, fpad2)

    along_z(apad, za)
    chunk_rows = 256

    def receivers(i, _):
        base = i * chunk_rows
        row = lax.broadcasted_iota(jnp.int32, (chunk_rows, nrec), 0) + base
        row_hot = jnp.where(row == rec_row, 1.0, 0.0).astype(jnp.bfloat16)
        res = lax.dot_general(row_hot, hot[...], (((1,), (1,)), ((), ())), preferred_element_type=jnp.float32)
        px = chunk_rows // ny
        rec0[pl.ds(i * px, px)] = (res[:, :nz] + res[:, nz:2 * nz]).reshape(px, ny, nz)
        rec1[pl.ds(i * px, px)] = (res[:, 2 * nz:3 * nz] + res[:, 3 * nz:]).reshape(px, ny, nz)
        return 0

    lax.fori_loop(0, nx * ny // chunk_rows, receivers, 0, unroll=2)
    loads[4].wait()
    sides(1).wait_recv()
    recv_faces(1, apad)
    q1 = qrecv[1]

    def adjoint(x):
        lap, near = laplace(apad, za, q1, x)
        c = courant[x]
        apad2[x + HALO, y0:y1, :] = 2.0 * near - far[x] + (c * c) * (lap + rec0[x])

    planes(adjoint, 0, 4)
    planes(adjoint, nx - 4, nx)
    send_faces(3, apad2)
    planes(adjoint, 4, nx - 4)
    pack(3, apad2)
    store_now = pltpu.make_async_copy(inner(apad2), anow_hbm.at[0], out_sem.at[0])
    store_now.start()

    along_z(fpad2, zf)
    sides(2).wait_recv()
    q2 = qrecv[2]

    def gradient(x):
        lap, _ = laplace(fpad2, zf, q2, x)
        g = (2.0 * weight) * courant[x] * (
            apad[x + HALO, y0:y1, :] * lap + apad2[x + HALO, y0:y1, :] * lapf[x])
        for s in range(shots):
            gbuf[s, x] = g[s * rows_y:(s + 1) * rows_y, :]

    for i in range(2):
        planes(gradient, *GRAD_CHUNKS[i])
        for d in range(1, shots):
            grads(i, d).start()
    recv_faces(2, fpad2)
    for i in range(2, 4):
        planes(gradient, *GRAD_CHUNKS[i])
        for d in range(1, shots):
            grads(i, d).start()

    along_z(apad2, za)
    sides(3).wait_recv()
    recv_faces(3, apad2)
    q3 = qrecv[3]

    def adjoint_back(x):
        lap, now = laplace(apad2, za, q3, x)
        c = courant[x]
        back[x] = 2.0 * now - apad[x + HALO, y0:y1, :] + (c * c) * (lap + rec1[x])

    planes(adjoint_back, 0, nx)
    store_back = pltpu.make_async_copy(back, aback_hbm.at[0], out_sem.at[1])
    store_back.start()

    stores = []
    for n, (buf, landing, copies, chunks, out) in enumerate((
            (ebuf, erecv, energy, ENERGY_CHUNKS, energy_hbm),
            (gbuf, grecv, grads, GRAD_CHUNKS, grad_hbm))):
        for i, (a, b) in enumerate(chunks):
            for d in range(1, shots):
                copies(i, d).wait_recv()

            def total(x, buf=buf, landing=landing):
                acc = buf[shot, x]
                for d in range(1, shots):
                    acc = acc + landing[d - 1, x]
                landing[0, x] = acc

            planes(total, a, b)
            store = pltpu.make_async_copy(landing.at[0, a:b], out.at[a:b], out_sem.at[2 + 4 * n + i])
            store.start()
            stores.append(store)

    for n, ref in enumerate((fpad, apad, fpad2, apad2)):
        sent_faces(n, ref)
        sides(n).wait_send()
    for i in range(4):
        for d in range(1, shots):
            energy(i, d).wait_send()
            grads(i, d).wait_send()
    store_now.wait()
    store_back.wait()
    for store in stores:
        store.wait()


def write_out(*refs):
    ins, outs, held, sem = refs[:4], refs[4:8], refs[8:12], refs[12]
    first = [pltpu.make_async_copy(ins[i], held[i], sem.at[i]) for i in range(4)]
    second = [pltpu.make_async_copy(held[i], outs[i], sem.at[4 + i]) for i in range(4)]
    for copy in first:
        copy.start()
    for arrive, leave in zip(first, second):
        arrive.wait()
        leave.start()
    for copy in second:
        copy.wait()


def shards(tiles, shots, *args):
    _, nx, ny, nz = args[2].shape
    nrec = args[8].shape[1]
    rows_y = ny // shots
    landings = max(shots - 1, 1)
    block = (nx, ny, nz)
    padded = (nx + 2 * HALO, ny + 2 * PAD, nz)
    f32 = jnp.float32
    anywhere = pl.BlockSpec(memory_space=pl.ANY)
    pinned = pl.BlockSpec(memory_space=pltpu.HBM)
    dma = pltpu.SemaphoreType.DMA
    scalars = jnp.concatenate([args[6], args[7], args[11]])
    held = pl.pallas_call(
        functools.partial(kernel, (tiles, shots, nx, ny, nz)),
        out_shape=(
            jax.ShapeDtypeStruct((nx, rows_y, nz), f32),
            jax.ShapeDtypeStruct((nx, rows_y, nz), f32),
            jax.ShapeDtypeStruct((1,) + block, f32),
            jax.ShapeDtypeStruct((1,) + block, f32),
        ),
        in_specs=[pinned] * 10,
        out_specs=(anywhere,) * 4,
        scratch_shapes=(
            [pltpu.VMEM(padded, f32)] * 4
            + [pltpu.VMEM(block, f32)] * 9
            + [pltpu.VMEM((shots, nx, rows_y, nz), f32)] * 2
            + [pltpu.VMEM((landings, nx, rows_y, nz), f32)] * 2
            + [
                pltpu.VMEM((2 * nz, 2 * nz), jnp.bfloat16),
                pltpu.VMEM((4, ny, nz), f32),
                pltpu.VMEM((4, ny, nz), f32),
                pltpu.VMEM((4 * nz, nrec), jnp.bfloat16),
                pltpu.SMEM(args[5].shape, f32),
                pltpu.SMEM((3,), jnp.int32),
                pltpu.VMEM(args[8].shape, jnp.int32),
                pltpu.VMEM(args[9].shape, f32),
                pltpu.SMEM(args[10].shape, f32),
                dma((12,)), dma((10,)), dma((8,)), dma((8,)), dma((4,)), dma((4,)),
                dma((4, landings)), dma((4, landings)), dma((4, landings)), dma((4, landings)),
            ]
        ),
        compiler_params=pltpu.CompilerParams(
            collective_id=0, has_side_effects=True, vmem_limit_bytes=60 * 1024 * 1024),
        cost_estimate=pl.CostEstimate(
            flops=130 * nx * ny * nz, bytes_accessed=32 * nx * ny * nz, transcendentals=0),
        name="adjoint_window",
    )(*args[:6], scalars, *args[8:11])
    return pl.pallas_call(
        write_out,
        out_shape=tuple(jax.ShapeDtypeStruct(h.shape, f32) for h in held),
        in_specs=[anywhere] * 4,
        out_specs=(pinned,) * 4,
        scratch_shapes=[pltpu.VMEM(h.shape, f32) for h in held] + [dma((8,))],
        compiler_params=pltpu.CompilerParams(vmem_limit_bytes=60 * 1024 * 1024),
        cost_estimate=pl.CostEstimate(flops=0, bytes_accessed=24 * nx * ny * nz, transcendentals=0),
        name="write_out",
    )(*held)


def solution(mesh):
    wave = P(("grp", "shot"), "tile", None, "gz")
    one = P(("grp", "shot"))
    in_specs = (P("tile", None, "gz"), wave, wave, wave, wave, P(), one, one,
                P(("grp", "shot"), None), P(("grp", "shot"), None, None), P(), one)
    out_specs = (P(("grp", "tile"), "shot", "gz"), P(("grp", "tile"), "shot", "gz"), wave, wave)
    body = functools.partial(shards, mesh.shape["tile"], mesh.shape["shot"])
    return jax.shard_map(body, mesh=mesh, in_specs=in_specs, out_specs=out_specs, check_vma=False)
```
